32 devices in a mesh: dp: 4 (over z), group: 8 (over y, x, core).
Axes of the slice: x: 2, y: 2, z: 4, core: 2. Of those that a mesh axis runs over, the one named last changes fastest.
Arguments:
- queries: float32 [8, 512, 4096], P('group', 'dp'), may hold values from -0.6 to 0.6
- passages: float32 [8, 512, 4096], P('group', 'dp'), may hold values from -0.09375 to 0.09375
- hard_ids: int32 [8, 512, 3], P('group', 'dp'), may hold values from 0 to 4095, as said below
Outputs:
- query_grad: float32 [8, 512, 4096], P('group', 'dp')
- passage_grad: float32 [8, 512, 4096], P('group', 'dp')
- losses: float32 [8, 512], P('group', 'dp')
The draws below stay inside these ranges and needn't reach their ends.
Inputs may be any that keep to these rules, and one draw needn't show every extreme that they name: `hard_ids`: passage g * 512 + i is held by the device that holds row i of sub-batch g. Of the 384 hard negatives of one device's queries, at most 12 are held by any one device, and some device holds exactly 12 of them; one device holds 12 of every device's hard negatives.
All inputs are finite; a program needn't handle non-finite values.
Results may differ from the reference program's by a relative error of at most 0.005.
Values may be sent and summed in bfloat16 or wider, within the bound.
No kernel may reach another device: no remote copies, remote signals or barrier semaphores. Data moves between devices by JAX's collectives and lax.ppermute only.
A program may use at most 128 MiB of HBM per device.

```python
import jax
import jax.numpy as jnp
from jax import lax

D = 4096
ROWS = 128
HARD = 3
SUBS = 8
BATCH = 512
CAP = 12


def hard_table(key):
    blocks = BATCH // ROWS
    owners = SUBS * blocks
    entries = HARD * ROWS
    common = jax.random.permutation(jax.random.fold_in(key, 11), owners)

    def one(requester):
        inner = jax.random.fold_in(jax.random.fold_in(key, 12), requester)
        first_key, second_key, third_key = jax.random.split(inner, 3)
        others = common[1:][jax.random.permutation(first_key, owners - 1)]
        order = jnp.concatenate([common[:1], others])
        slots = jax.random.permutation(second_key, entries)
        owner = order[slots // CAP]
        local_row = jax.random.randint(third_key, (entries,), 0, ROWS)
        block = owner // SUBS
        sub_index = owner % SUBS
        numbers = sub_index * BATCH + block * ROWS + local_row
        return numbers.reshape(ROWS, HARD)
    table = jax.vmap(one)(jnp.arange(owners))
    table = table.reshape(blocks, SUBS, ROWS, HARD).transpose(1, 0, 2, 3).reshape(SUBS, BATCH, HARD)
    return table.astype(jnp.int32)


def passage_table(key):
    shape = (SUBS, BATCH, D)
    passage_sigma = 1.0 / D ** 0.5
    values = jax.random.normal(jax.random.fold_in(key, 22), shape, jnp.float32) * passage_sigma
    values = jnp.clip(values, -6.0 * passage_sigma, 6.0 * passage_sigma)
    return values


def draw_passages(key, part):
    return passage_table(key)


def draw_hard_ids(key, part):
    return hard_table(key)


def draw_queries(key, part):
    passages = passage_table(key)
    numbers = hard_table(key)
    flat = passages.reshape(SUBS * BATCH, D)
    signal = passages
    for which in range(HARD):
        signal = signal + flat[numbers[:, :, which]]
    weight = jax.random.uniform(jax.random.fold_in(key, 31), (SUBS, BATCH, 1), jnp.float32, 0.16, 0.26)
    noise = jax.random.normal(jax.random.fold_in(key, 32), (SUBS, BATCH, D), jnp.float32) * 0.06
    noise = jnp.clip(noise, -0.36, 0.36)
    values = noise + weight * signal
    return jnp.clip(values, -0.6, 0.6)


def setup_inputs(seed: int = 0) -> dict:
    key_of = jax.random.split(jax.random.key(seed), 4)
    return {
        "queries": draw_queries(jax.random.fold_in(key_of[3], 71), 0),
        "passages": draw_passages(jax.random.fold_in(key_of[3], 71), 0),
        "hard_ids": draw_hard_ids(jax.random.fold_in(key_of[3], 71), 0),
    }


inverse_temp = 50.0


def reference(queries, passages, hard_ids):
    sub_count, batch_rows, features = queries.shape
    query_low = queries.astype(jnp.bfloat16)
    passage_low = passages.astype(jnp.bfloat16)
    flat_low = passage_low.reshape(sub_count * batch_rows, features)

    def one_sub(index):
        query_part = query_low[index]
        passage_part = passage_low[index]
        wanted = hard_ids[index]
        scores = jnp.dot(query_part, passage_part.T, preferred_element_type=jnp.float32) * inverse_temp
        hard_rows = flat_low[wanted]
        query_wide = query_part.astype(jnp.float32)
        hard_wide = hard_rows.astype(jnp.float32)
        hard_scores = jnp.sum(query_wide[:, None, :] * hard_wide, axis=2) * inverse_temp
        highest = jnp.maximum(jnp.max(scores, axis=1), jnp.max(hard_scores, axis=1))
        totals = jnp.sum(jnp.exp(scores - highest[:, None]), axis=1) + jnp.sum(jnp.exp(hard_scores - highest[:, None]), axis=1)
        normal = highest + jnp.log(totals)
        losses = normal - jnp.diagonal(scores)
        coeff = (jnp.exp(scores - normal[:, None]) - jnp.eye(batch_rows, dtype=jnp.float32)).astype(jnp.bfloat16)
        hard_coeff = jnp.exp(hard_scores - normal[:, None])
        query_grad = inverse_temp * (jnp.dot(coeff, passage_part, preferred_element_type=jnp.float32) + jnp.sum(hard_coeff[:, :, None] * hard_wide, axis=1))
        cycle_grad = inverse_temp * jnp.dot(coeff.T, query_part, preferred_element_type=jnp.float32)
        hard_grad = (inverse_temp * hard_coeff[:, :, None] * query_wide[:, None, :]).astype(jnp.bfloat16)
        return query_grad, cycle_grad, losses, hard_grad

    query_grad, cycle_grad, losses, hard_grad = lax.map(one_sub, jnp.arange(sub_count))

    def add_rows(carry, item):
        rows_low, wanted = item
        carry = carry.at[wanted.reshape(-1)].add(rows_low.reshape(-1, features).astype(jnp.float32))
        return carry, None

    start_sum = jnp.zeros((sub_count * batch_rows, features), jnp.float32)
    extra, unused = lax.scan(add_rows, start_sum, (hard_grad, hard_ids))
    passage_grad = cycle_grad + extra.reshape(sub_count, batch_rows, features)
    return query_grad, passage_grad, losses
```

```python
import jax
import jax.numpy as jnp
from jax import lax
from jax.sharding import PartitionSpec as P

inverse_temp = 50.0
parts = 2


def first_hop(block, count):
    upward = [(i, i + 1) for i in range(count - 1)]
    downward = [(i + 1, i) for i in range(count - 1)]
    up = {1: lax.ppermute(block, "dp", upward)}
    down = {1: lax.ppermute(block, "dp", downward)}
    if count > 2:
        far = lax.ppermute(block, "dp", [(0, count - 1), (count - 1, 0)])
        up[count - 1] = down[count - 1] = far
    return up, down


def other_hops(block, up, down, count):
    upward = [(i, i + 1) for i in range(count - 1)]
    downward = [(i + 1, i) for i in range(count - 1)]
    for hop in range(2, count - 1):
        up[hop] = lax.ppermute(up[hop - 1], "dp", upward)
        down[hop] = lax.ppermute(down[hop - 1], "dp", downward)
    me = lax.axis_index("dp")
    blocks = [block]
    for k in range(1, count):
        blocks.append(jnp.where(me >= k, up[k], down[count - k]))
    return jnp.concatenate(blocks, axis=0)


def per_device(queries, passages, hard_ids):
    row_count, features = queries.shape[1:]
    hard = hard_ids.shape[2]
    dp_count = lax.axis_size("dp")
    group_count = lax.axis_size("group")
    devices = dp_count * group_count
    me = lax.axis_index("dp")
    my_group = lax.axis_index("group")
    batch_rows = row_count * dp_count
    entries = row_count * hard
    capacity = (entries + devices - 1) // devices
    slots = devices * capacity
    width = features // parts

    passage_low = passages[0].astype(jnp.bfloat16)
    query_low = queries[0].astype(jnp.bfloat16)

    stream = [x[:, i * width : (i + 1) * width] for x in (passage_low, query_low) for i in range(parts)]
    gathered = []
    before = None
    for block in stream:
        sent = block if before is None else lax.optimization_barrier((block,) + before)[0]
        up, down = first_hop(sent, dp_count)
        before = (up[1], down[1])
        gathered.append(other_hops(block, up, down, dp_count))
    passage_parts, query_parts = gathered[:parts], gathered[parts:]

    ids = hard_ids[0].T.reshape(entries)
    owner_group = ids // batch_rows
    owner_dp = ids % batch_rows // row_count
    owner = owner_group * dp_count + owner_dp
    order = jnp.arange(entries)
    earlier = (order[None, :] < order[:, None]) & (owner[None, :] == owner[:, None])
    rank = jnp.sum(earlier.astype(jnp.int32), axis=1)
    slot = owner * capacity + rank
    place = jnp.arange(slots)[:, None] == slot[None, :]
    query_row = jnp.sum(jnp.where(place, order[None, :] % row_count + 1, 0), axis=1) - 1
    passage_row = jnp.sum(jnp.where(place, ids[None, :] % row_count + 1, 0), axis=1) - 1

    def place_of(rows, dp_index):
        return jnp.where(rows >= 0, (me - dp_index) % dp_count * row_count + rows, -1)

    def one_hot(positions, count):
        return (positions[:, None] == jnp.arange(count)[None, :]).astype(jnp.bfloat16)

    asked = lax.all_to_all(
        passage_row.reshape(group_count, dp_count * capacity), "group", split_axis=0, concat_axis=0, tiled=True
    ).reshape(group_count, dp_count, capacity)
    dp_indices = jnp.arange(dp_count)
    fetch_place = place_of(asked, dp_indices[None, :, None]).reshape(slots)
    told = lax.all_to_all(
        query_row.reshape(group_count, dp_count, capacity).transpose(1, 0, 2).reshape(dp_count, group_count * capacity),
        "dp",
        split_axis=0,
        concat_axis=0,
        tiled=True,
    ).reshape(dp_count, group_count, capacity)
    push_place = place_of(told, dp_indices[:, None, None]).transpose(1, 0, 2).reshape(slots)

    def send_rows(positions, table):
        chosen = jnp.dot(one_hot(positions, batch_rows), table, preferred_element_type=jnp.float32).astype(
            jnp.bfloat16
        )
        moved = lax.all_to_all(
            chosen.reshape(group_count, dp_count * capacity, -1), "group", split_axis=0, concat_axis=0, tiled=True
        )
        return moved.reshape(slots, -1)

    hard_parts = [send_rows(fetch_place, table) for table in passage_parts]
    pushed_parts = [send_rows(push_place, table) for table in query_parts]

    def inner(left, rights):
        total = 0.0
        for i, right in enumerate(rights):
            total = total + lax.dot_general(
                left[:, i * width : (i + 1) * width],
                right,
                (((1,), (1,)), ((), ())),
                preferred_element_type=jnp.float32,
            )
        return total * inverse_temp

    diagonal = jnp.arange(row_count)[:, None] == jnp.arange(batch_rows)[None, :]
    scores = inner(query_low, passage_parts)
    owned = query_row[None, :] == jnp.arange(row_count)[:, None]
    hard_scores = jnp.where(owned, inner(query_low, hard_parts), -jnp.inf)
    highest = jnp.maximum(jnp.max(scores, axis=1), jnp.max(hard_scores, axis=1))
    totals = jnp.sum(jnp.exp(scores - highest[:, None]), axis=1) + jnp.sum(
        jnp.exp(hard_scores - highest[:, None]), axis=1
    )
    normal = highest + jnp.log(totals)
    losses = normal - jnp.sum(jnp.where(diagonal, scores, 0.0), axis=1)
    coeff = (jnp.exp(scores - normal[:, None]) - diagonal.astype(jnp.float32)).astype(jnp.bfloat16)
    hard_coeff = jnp.exp(hard_scores - normal[:, None])

    note = jnp.concatenate(
        [
            x.reshape(group_count, dp_count, capacity).transpose(1, 0, 2).reshape(devices, capacity)
            for x in (passage_row.astype(jnp.float32), jnp.sum(hard_coeff, axis=0))
        ]
        + [jnp.broadcast_to(normal[None, :], (devices, row_count))],
        axis=1,
    )
    notes = lax.all_to_all(note, ("dp", "group"), split_axis=0, concat_axis=0, tiled=True)
    notes = notes.reshape(dp_count, group_count, 2 * capacity + row_count)
    owned_row = notes[:, :, :capacity].transpose(1, 0, 2).reshape(slots)
    owned_coeff = notes[:, :, capacity : 2 * capacity].transpose(1, 0, 2).reshape(slots)
    normals = lax.dynamic_index_in_dim(notes[:, :, 2 * capacity :], my_group, axis=1, keepdims=False)
    normals = normals[(me - dp_indices) % dp_count].reshape(batch_rows)

    hard_low = hard_coeff.astype(jnp.bfloat16)
    query_grad = jnp.concatenate(
        [
            inverse_temp
            * (
                jnp.dot(coeff, table, preferred_element_type=jnp.float32)
                + jnp.dot(hard_low, rows, preferred_element_type=jnp.float32)
            )
            for table, rows in zip(passage_parts, hard_parts)
        ],
        axis=1,
    )

    back_scores = inner(passage_low, query_parts)
    back_coeff = (jnp.exp(back_scores - normals[None, :]) - diagonal.astype(jnp.float32)).astype(jnp.bfloat16)
    spread = jnp.where(
        jnp.arange(row_count).astype(jnp.float32)[:, None] == owned_row[None, :], owned_coeff[None, :], 0.0
    ).astype(jnp.bfloat16)
    passage_grad = jnp.concatenate(
        [
            inverse_temp
            * (
                jnp.dot(back_coeff, table, preferred_element_type=jnp.float32)
                + jnp.dot(spread, rows, preferred_element_type=jnp.float32)
            )
            for table, rows in zip(query_parts, pushed_parts)
        ],
        axis=1,
    )
    return (query_grad[None], passage_grad[None], losses[None])


def solution(mesh):
    return jax.shard_map(
        per_device,
        mesh=mesh,
        in_specs=(P("group", "dp", None), P("group", "dp", None), P("group", "dp", None)),
        out_specs=(P("group", "dp", None), P("group", "dp", None), P("group", "dp")),
        check_vma=False,
    )
```

```python
import jax
import jax.numpy as jnp
from jax import lax
from jax.sharding import PartitionSpec as P

inverse_temp = 50.0
pieces = 2


def matmul(a, b, left, right):
    return lax.dot_general(a, b, (((left,), (right,)), ((), ())), preferred_element_type=jnp.float32)


def per_device(queries, passages, hard_ids):
    row_count, features = queries.shape[1:]
    hard = hard_ids.shape[2]
    dp_count = lax.axis_size("dp")
    group_count = lax.axis_size("group")
    devices = dp_count * group_count
    me = lax.axis_index("dp")
    my_group = lax.axis_index("group")
    batch_rows = row_count * dp_count
    entries = row_count * hard
    capacity = (entries + devices - 1) // devices
    slots = devices * capacity
    piece_rows = row_count // pieces

    query_low = queries[0].astype(jnp.bfloat16)
    passage_low = passages[0].astype(jnp.bfloat16)

    gathered = []
    for i in range(pieces):
        piece = query_low[i * piece_rows : (i + 1) * piece_rows]
        gathered.append(lax.all_gather(piece, "dp", axis=0, tiled=True))

    ids = hard_ids[0].T.reshape(entries)
    owner_group = ids // batch_rows
    owner_dp = ids % batch_rows // row_count
    owner = owner_dp * group_count + owner_group
    order = jnp.arange(entries)
    earlier = (order[None, :] < order[:, None]) & (owner[None, :] == owner[:, None])
    rank = jnp.sum(earlier.astype(jnp.int32), axis=1)
    slot = owner * capacity + rank
    placed = jnp.arange(slots)[:, None] == slot[None, :]
    query_row = jnp.sum(jnp.where(placed, order[None, :] % row_count + 1, 0), axis=1) - 1
    passage_row = jnp.sum(jnp.where(placed, ids[None, :] % row_count + 1, 0), axis=1) - 1

    plane = group_count * capacity
    request = jnp.concatenate(
        [
            passage_row.reshape(dp_count, group_count, capacity),
            jnp.broadcast_to(query_row.reshape(dp_count, 1, plane), (dp_count, group_count, plane)),
        ],
        axis=2,
    ).reshape(devices, capacity + plane)
    request = lax.all_to_all(request, ("dp", "group"), split_axis=0, concat_axis=0, tiled=True)
    request = request.reshape(dp_count, group_count, capacity + plane)
    sent_row = request[:, :, :capacity].transpose(1, 0, 2).reshape(slots)
    wanting = lax.dynamic_index_in_dim(request[:, :, capacity:], my_group, axis=1, keepdims=False)
    wanting = wanting.reshape(dp_count, group_count, capacity).transpose(1, 0, 2).reshape(slots)
    wanting_dp = jnp.arange(slots) // capacity % dp_count

    select = (jnp.arange(row_count)[:, None] == sent_row[None, :]).astype(jnp.bfloat16)

    def exchange(rows):
        rows = rows.astype(jnp.bfloat16).reshape(group_count, dp_count * capacity, features)
        return lax.all_to_all(rows, "group", split_axis=0, concat_axis=0, tiled=True).reshape(slots, features)

    table = jnp.concatenate([passage_low, exchange(matmul(select, passage_low, 0, 0))], axis=0)

    weights, losses, query_grad = [], [], []
    share = None
    for i, piece in enumerate(gathered):
        if share is not None:
            piece = lax.optimization_barrier((piece, share))[0]
        first = i * piece_rows
        count = dp_count * piece_rows
        row = jnp.arange(count)[:, None]
        local = wanting - first
        target = jnp.where((local >= 0) & (local < piece_rows), wanting_dp * piece_rows + local, -1)
        mine = jnp.arange(row_count) - first
        positive = jnp.where((mine >= 0) & (mine < piece_rows), me * piece_rows + mine, -1)
        positive = row == jnp.concatenate([positive, jnp.full((slots,), -1, jnp.int32)])[None, :]
        masked = row != jnp.concatenate([jnp.broadcast_to(row[0], (row_count,)) * 0 - 1, target])[None, :]
        masked = masked & (jnp.arange(row_count + slots)[None, :] >= row_count)
        scores = jnp.where(masked, -jnp.inf, matmul(piece, table, 1, 1) * inverse_temp)
        highest = jnp.max(scores, axis=1)
        total = jnp.sum(jnp.exp(scores - highest[:, None]), axis=1)
        stats = jnp.broadcast_to(jnp.stack([highest, total])[None], (dp_count, 2, count))
        stats = lax.all_to_all(stats, "dp", split_axis=0, concat_axis=0, tiled=True)
        highest = jnp.max(stats[:, 0], axis=0)
        normal = highest + jnp.log(jnp.sum(stats[:, 1] * jnp.exp(stats[:, 0] - highest[None, :]), axis=0))
        loss = normal - jnp.sum(jnp.where(positive, scores, 0.0), axis=1)
        losses.append(lax.dynamic_slice_in_dim(loss, me * piece_rows, piece_rows, axis=0))
        weight = jnp.exp(scores - normal[:, None]) - positive.astype(jnp.float32)
        weights.append(weight.astype(jnp.bfloat16))
        share = (matmul(weights[-1], table, 1, 0) * inverse_temp).astype(jnp.bfloat16)
        query_grad.append(lax.psum_scatter(share, "dp", scatter_dimension=0, tiled=True))

    weights = jnp.concatenate(weights, axis=0)
    everything = jnp.concatenate(gathered, axis=0)
    passage_grad = matmul(weights[:, :row_count], everything, 0, 0)
    hard_grad = matmul(weights[:, row_count:], everything, 0, 0) * inverse_temp
    passage_grad = passage_grad * inverse_temp + matmul(select, exchange(hard_grad), 1, 0)
    query_grad = jnp.concatenate(query_grad, axis=0).astype(jnp.float32)
    return (query_grad[None], passage_grad[None], jnp.concatenate(losses)[None])


def solution(mesh):
    return jax.shard_map(
        per_device,
        mesh=mesh,
        in_specs=(P("group", "dp", None), P("group", "dp", None), P("group", "dp", None)),
        out_specs=(P("group", "dp", None), P("group", "dp", None), P("group", "dp")),
        check_vma=False,
    )
```

```python
import jax
import jax.numpy as jnp
from jax import lax
from jax.sharding import PartitionSpec as P

inverse_temp = 50.0
pieces = 1


def matmul(a, b, left, right):
    return lax.dot_general(a, b, (((left,), (right,)), ((), ())), preferred_element_type=jnp.float32)


def per_device(queries, passages, hard_ids):
    row_count, features = queries.shape[1:]
    hard = hard_ids.shape[2]
    dp_count = lax.axis_size("dp")
    group_count = lax.axis_size("group")
    devices = dp_count * group_count
    me = lax.axis_index("dp")
    my_group = lax.axis_index("group")
    batch_rows = row_count * dp_count
    entries = row_count * hard
    capacity = (entries + devices - 1) // devices
    slots = devices * capacity
    piece_rows = row_count // pieces

    query_low = queries[0].astype(jnp.bfloat16)
    passage_low = passages[0].astype(jnp.bfloat16)

    gathered = []
    for i in range(pieces):
        piece = query_low[i * piece_rows : (i + 1) * piece_rows]
        gathered.append(lax.all_gather(piece, "dp", axis=0, tiled=True))

    ids = hard_ids[0].T.reshape(entries)
    owner_group = ids // batch_rows
    owner_dp = ids % batch_rows // row_count
    owner = owner_dp * group_count + owner_group
    order = jnp.arange(entries)
    earlier = (order[None, :] < order[:, None]) & (owner[None, :] == owner[:, None])
    rank = jnp.sum(earlier.astype(jnp.int32), axis=1)
    slot = owner * capacity + rank
    placed = jnp.arange(slots)[:, None] == slot[None, :]
    query_row = jnp.sum(jnp.where(placed, order[None, :] % row_count + 1, 0), axis=1) - 1
    passage_row = jnp.sum(jnp.where(placed, ids[None, :] % row_count + 1, 0), axis=1) - 1

    plane = group_count * capacity
    request = jnp.concatenate(
        [
            passage_row.reshape(dp_count, group_count, capacity),
            jnp.broadcast_to(query_row.reshape(dp_count, 1, plane), (dp_count, group_count, plane)),
        ],
        axis=2,
    ).reshape(devices, capacity + plane)
    request = lax.all_to_all(request, ("dp", "group"), split_axis=0, concat_axis=0, tiled=True)
    request = request.reshape(dp_count, group_count, capacity + plane)
    sent_row = request[:, :, :capacity].transpose(1, 0, 2).reshape(slots)
    wanting = lax.dynamic_index_in_dim(request[:, :, capacity:], my_group, axis=1, keepdims=False)
    wanting = wanting.reshape(dp_count, group_count, capacity).transpose(1, 0, 2).reshape(slots)
    wanting_dp = jnp.arange(slots) // capacity % dp_count

    select = (jnp.arange(row_count)[:, None] == sent_row[None, :]).astype(jnp.bfloat16)

    def exchange(rows):
        rows = rows.astype(jnp.bfloat16).reshape(group_count, dp_count * capacity, features)
        return lax.all_to_all(rows, "group", split_axis=0, concat_axis=0, tiled=True).reshape(slots, features)

    table = jnp.concatenate([passage_low, exchange(matmul(select, passage_low, 0, 0))], axis=0)

    weights, losses, query_grad = [], [], []
    share = None
    for i, piece in enumerate(gathered):
        if share is not None:
            piece = lax.optimization_barrier((piece, share))[0]
        first = i * piece_rows
        count = dp_count * piece_rows
        row = jnp.arange(count)[:, None]
        local = wanting - first
        target = jnp.where((local >= 0) & (local < piece_rows), wanting_dp * piece_rows + local, -1)
        mine = jnp.arange(row_count) - first
        positive = jnp.where((mine >= 0) & (mine < piece_rows), me * piece_rows + mine, -1)
        positive = row == jnp.concatenate([positive, jnp.full((slots,), -1, jnp.int32)])[None, :]
        masked = row != jnp.concatenate([jnp.broadcast_to(row[0], (row_count,)) * 0 - 1, target])[None, :]
        masked = masked & (jnp.arange(row_count + slots)[None, :] >= row_count)
        scores = jnp.where(masked, -jnp.inf, matmul(piece, table, 1, 1) * inverse_temp)
        highest = jnp.max(scores, axis=1)
        total = jnp.sum(jnp.exp(scores - highest[:, None]), axis=1)
        stats = jnp.broadcast_to(jnp.stack([highest, total])[None], (dp_count, 2, count))
        stats = lax.all_to_all(stats, "dp", split_axis=0, concat_axis=0, tiled=True)
        highest = jnp.max(stats[:, 0], axis=0)
        normal = highest + jnp.log(jnp.sum(stats[:, 1] * jnp.exp(stats[:, 0] - highest[None, :]), axis=0))
        loss = normal - jnp.sum(jnp.where(positive, scores, 0.0), axis=1)
        losses.append(lax.dynamic_slice_in_dim(loss, me * piece_rows, piece_rows, axis=0))
        weight = jnp.exp(scores - normal[:, None]) - positive.astype(jnp.float32)
        weights.append(weight.astype(jnp.bfloat16))
        share = (matmul(weights[-1], table, 1, 0) * inverse_temp).astype(jnp.bfloat16)
        query_grad.append(lax.psum_scatter(share, "dp", scatter_dimension=0, tiled=True))

    weights = jnp.concatenate(weights, axis=0)
    everything = jnp.concatenate(gathered, axis=0)
    passage_grad = matmul(weights[:, :row_count], everything, 0, 0)
    hard_grad = matmul(weights[:, row_count:], everything, 0, 0) * inverse_temp
    passage_grad = passage_grad * inverse_temp + matmul(select, exchange(hard_grad), 1, 0)
    query_grad = jnp.concatenate(query_grad, axis=0).astype(jnp.float32)
    return (query_grad[None], passage_grad[None], jnp.concatenate(losses)[None])


def solution(mesh):
    return jax.shard_map(
        per_device,
        mesh=mesh,
        in_specs=(P("group", "dp", None), P("group", "dp", None), P("group", "dp", None)),
        out_specs=(P("group", "dp", None), P("group", "dp", None), P("group", "dp")),
        check_vma=False,
    )
```

```python
import jax
import jax.numpy as jnp
from jax import lax
from jax.sharding import PartitionSpec as P

inverse_temp = 50.0
direct_part = 4


def ways(step, count):
    return [(i, i + 1) for i in range(step - 1, count - 1)], [(i + 1, i) for i in range(count - step)]


def scatter_begin(share, me, count):
    rows = share.shape[0] // count

    def part(index):
        return lax.dynamic_slice_in_dim(share, index * rows, rows, axis=0)

    terms = [part(me)]
    up, down = None, None
    for step in range(max(count - 2, 1), 0, -1):
        low, high = part((me - step) % count), part((me + step) % count)
        if up is not None:
            low = low.astype(jnp.float32), down
            high = high.astype(jnp.float32), up
        if step > 1:
            above, below = ways(step, count)
            if up is not None:
                low, high = (added(*x) for x in (low, high))
            down = lax.ppermute(low, "dp", [(j, i) for i, j in above])
            up = lax.ppermute(high, "dp", [(j, i) for i, j in below])
    if count > 2:
        terms.append(lax.ppermute(part(count - 1 - me), "dp", [(0, count - 1), (count - 1, 0)]))
    return terms, low, high


def added(kept, came):
    return (kept + came.astype(jnp.float32)).astype(jnp.bfloat16)


def scatter_end(terms, low, high, count):
    low, high = (added(*x) if isinstance(x, tuple) else x for x in (low, high))
    above, below = ways(1, count)
    down = lax.ppermute(low, "dp", [(j, i) for i, j in above])
    up = lax.ppermute(high, "dp", [(j, i) for i, j in below])
    return sum(term.astype(jnp.float32) for term in terms + [up, down])


def matmul(a, b, left, right):
    return lax.dot_general(a, b, (((left,), (right,)), ((), ())), preferred_element_type=jnp.float32)


def per_device(queries, passages, hard_ids):
    row_count, features = queries.shape[1:]
    hard = hard_ids.shape[2]
    dp_count = lax.axis_size("dp")
    group_count = lax.axis_size("group")
    devices = dp_count * group_count
    me = lax.axis_index("dp")
    my_group = lax.axis_index("group")
    batch_rows = row_count * dp_count
    entries = row_count * hard
    capacity = (entries + devices - 1) // devices
    slots = devices * capacity

    query_low = queries[0].astype(jnp.bfloat16)
    passage_low = passages[0].astype(jnp.bfloat16)

    everything = lax.all_gather(query_low, "dp", axis=0, tiled=True)

    ids = hard_ids[0].T.reshape(entries)
    owner_group = ids // batch_rows
    owner_dp = ids % batch_rows // row_count
    owner = owner_dp * group_count + owner_group
    order = jnp.arange(entries)
    earlier = (order[None, :] < order[:, None]) & (owner[None, :] == owner[:, None])
    rank = jnp.sum(earlier.astype(jnp.int32), axis=1)
    slot = owner * capacity + rank
    placed = jnp.arange(slots)[:, None] == slot[None, :]
    query_row = jnp.sum(jnp.where(placed, order[None, :] % row_count + 1, 0), axis=1) - 1
    passage_row = jnp.sum(jnp.where(placed, ids[None, :] % row_count + 1, 0), axis=1) - 1

    plane = group_count * capacity
    request = jnp.concatenate(
        [
            passage_row.reshape(dp_count, group_count, capacity),
            jnp.broadcast_to(query_row.reshape(dp_count, 1, plane), (dp_count, group_count, plane)),
        ],
        axis=2,
    ).reshape(devices, capacity + plane)
    request = lax.all_to_all(request, ("dp", "group"), split_axis=0, concat_axis=0, tiled=True)
    request = request.reshape(dp_count, group_count, capacity + plane)
    sent_row = request[:, :, :capacity].transpose(1, 0, 2).reshape(slots)
    wanting = lax.dynamic_index_in_dim(request[:, :, capacity:], my_group, axis=1, keepdims=False)
    wanting = wanting.reshape(dp_count, group_count, capacity).transpose(1, 0, 2).reshape(slots)
    wanting_dp = jnp.arange(slots) // capacity % dp_count

    select = (jnp.arange(row_count)[:, None] == sent_row[None, :]).astype(jnp.bfloat16)

    def exchange(rows):
        rows = rows.astype(jnp.bfloat16).reshape(group_count, dp_count * capacity, features)
        return lax.all_to_all(rows, "group", split_axis=0, concat_axis=0, tiled=True).reshape(slots, features)

    table = jnp.concatenate([passage_low, exchange(matmul(select, passage_low, 0, 0))], axis=0)

    row = jnp.arange(batch_rows)[:, None]
    target = jnp.where(wanting >= 0, wanting_dp * row_count + wanting, -1)
    positive = me * row_count + jnp.arange(row_count)
    positive = row == jnp.pad(positive, (0, slots), constant_values=-1)[None, :]
    masked = row != jnp.pad(target, (row_count, 0))[None, :]
    masked = masked & (jnp.arange(row_count + slots)[None, :] >= row_count)
    scores = jnp.where(masked, -jnp.inf, matmul(everything, lax.optimization_barrier(table.T), 1, 0) * inverse_temp)
    highest = jnp.max(scores, axis=1)
    total = jnp.sum(jnp.exp(scores - highest[:, None]), axis=1)
    stats = jnp.broadcast_to(jnp.stack([highest, total])[None], (dp_count, 2, batch_rows))
    stats = lax.all_to_all(stats, "dp", split_axis=0, concat_axis=0, tiled=True)
    highest = jnp.max(stats[:, 0], axis=0)
    normal = highest + jnp.log(jnp.sum(stats[:, 1] * jnp.exp(stats[:, 0] - highest[None, :]), axis=0))
    losses = normal - jnp.sum(jnp.where(positive, scores, 0.0), axis=1)
    losses = lax.dynamic_slice_in_dim(losses, me * row_count, row_count, axis=0)
    weights = jnp.exp(scores - normal[:, None]) - positive.astype(jnp.float32)
    weights = weights.astype(jnp.bfloat16)

    direct = features // direct_part
    share = (matmul(weights, table[:, direct:], 1, 0) * inverse_temp).astype(jnp.bfloat16)
    later = lax.psum_scatter(share, "dp", scatter_dimension=0, tiled=True)
    weights, share = lax.optimization_barrier((weights, share))
    ahead = (matmul(weights, table[:, :direct], 1, 0) * inverse_temp).astype(jnp.bfloat16)
    ahead = scatter_end(*scatter_begin(ahead, me, dp_count), dp_count)

    passage_grad = matmul(weights[:, :row_count], everything, 0, 0)
    hard_grad = matmul(weights[:, row_count:], everything, 0, 0) * inverse_temp
    passage_grad = passage_grad * inverse_temp + matmul(select, exchange(hard_grad), 1, 0)
    query_grad = jnp.pad(ahead, ((0, 0), (0, features - direct)))
    query_grad, later, passage_grad = lax.optimization_barrier((query_grad, later, passage_grad))
    query_grad = lax.dynamic_update_slice(query_grad, later.astype(jnp.float32), (0, direct))
    return (query_grad[None], passage_grad[None], losses[None])


def solution(mesh):
    return jax.shard_map(
        per_device,
        mesh=mesh,
        in_specs=(P("group", "dp", None), P("group", "dp", None), P("group", "dp", None)),
        out_specs=(P("group", "dp", None), P("group", "dp", None), P("group", "dp")),
        check_vma=False,
    )
```

```python
import jax
import jax.numpy as jnp
from jax import lax
from jax.sharding import PartitionSpec as P

inverse_temp = 50.0
later_part = 8


def ways(step, count):
    return [(i, i + 1) for i in range(step - 1, count - 1)], [(i + 1, i) for i in range(count - step)]


def send_direct(block, count):
    return [lax.ppermute(block, "dp", [(i, (i + step) % count) for i in range(count)]) for step in range(1, count)]


def in_order(block, moved, me, count):
    rows = block.shape[0]
    whole = jnp.zeros((rows * count, block.shape[1]), block.dtype)
    for step, x in enumerate([block] + moved):
        whole = lax.dynamic_update_slice_in_dim(whole, x, (me - step) % count * rows, axis=0)
    return whole


def scatter_begin(share, me, count):
    rows = share.shape[0] // count

    def part(index):
        return lax.dynamic_slice_in_dim(share, index * rows, rows, axis=0)

    terms = [part(me)]
    up, down = None, None
    for step in range(max(count - 2, 1), 0, -1):
        low, high = part((me - step) % count), part((me + step) % count)
        if up is not None:
            low = low.astype(jnp.float32), down
            high = high.astype(jnp.float32), up
        if step > 1:
            above, below = ways(step, count)
            if up is not None:
                low, high = (added(*x) for x in (low, high))
            down = lax.ppermute(low, "dp", [(j, i) for i, j in above])
            up = lax.ppermute(high, "dp", [(j, i) for i, j in below])
    if count > 2:
        terms.append(lax.ppermute(part(count - 1 - me), "dp", [(0, count - 1), (count - 1, 0)]))
    return terms, low, high


def added(kept, came):
    return (kept + came.astype(jnp.float32)).astype(jnp.bfloat16)


def scatter_end(terms, low, high, count):
    low, high = (added(*x) if isinstance(x, tuple) else x for x in (low, high))
    above, below = ways(1, count)
    down = lax.ppermute(low, "dp", [(j, i) for i, j in above])
    up = lax.ppermute(high, "dp", [(j, i) for i, j in below])
    return sum(term.astype(jnp.float32) for term in terms + [up, down])


def matmul(a, b, left, right):
    return lax.dot_general(a, b, (((left,), (right,)), ((), ())), preferred_element_type=jnp.float32)


def per_device(queries, passages, hard_ids):
    row_count, features = queries.shape[1:]
    hard = hard_ids.shape[2]
    dp_count = lax.axis_size("dp")
    group_count = lax.axis_size("group")
    devices = dp_count * group_count
    me = lax.axis_index("dp")
    my_group = lax.axis_index("group")
    batch_rows = row_count * dp_count
    entries = row_count * hard
    capacity = (entries + devices - 1) // devices
    slots = devices * capacity

    ahead = row_count - row_count // later_part
    query_ahead = queries[0, :ahead].astype(jnp.bfloat16)
    query_later = queries[0, ahead:].astype(jnp.bfloat16)
    passage_low = passages[0].astype(jnp.bfloat16)

    piece_ahead = lax.all_gather(query_ahead, "dp", axis=0, tiled=True)
    piece_later = in_order(query_later, send_direct(query_later, dp_count), me, dp_count)
    gathered = [piece_ahead, piece_later]
    starts = [(0, ahead), (ahead, row_count)]

    ids = hard_ids[0].T.reshape(entries)
    owner_group = ids // batch_rows
    owner_dp = ids % batch_rows // row_count
    owner = owner_dp * group_count + owner_group
    order = jnp.arange(entries)
    earlier = (order[None, :] < order[:, None]) & (owner[None, :] == owner[:, None])
    rank = jnp.sum(earlier.astype(jnp.int32), axis=1)
    slot = owner * capacity + rank
    placed = jnp.arange(slots)[:, None] == slot[None, :]
    query_row = jnp.sum(jnp.where(placed, order[None, :] % row_count + 1, 0), axis=1) - 1
    passage_row = jnp.sum(jnp.where(placed, ids[None, :] % row_count + 1, 0), axis=1) - 1

    plane = group_count * capacity
    request = jnp.concatenate(
        [
            passage_row.reshape(dp_count, group_count, capacity),
            jnp.broadcast_to(query_row.reshape(dp_count, 1, plane), (dp_count, group_count, plane)),
        ],
        axis=2,
    ).reshape(devices, capacity + plane)
    request = lax.all_to_all(request, ("dp", "group"), split_axis=0, concat_axis=0, tiled=True)
    request = request.reshape(dp_count, group_count, capacity + plane)
    sent_row = request[:, :, :capacity].transpose(1, 0, 2).reshape(slots)
    wanting = lax.dynamic_index_in_dim(request[:, :, capacity:], my_group, axis=1, keepdims=False)
    wanting = wanting.reshape(dp_count, group_count, capacity).transpose(1, 0, 2).reshape(slots)
    wanting_dp = jnp.arange(slots) // capacity % dp_count

    select = (jnp.arange(row_count)[:, None] == sent_row[None, :]).astype(jnp.bfloat16)

    def exchange(rows):
        rows = rows.astype(jnp.bfloat16).reshape(group_count, dp_count * capacity, features)
        return lax.all_to_all(rows, "group", split_axis=0, concat_axis=0, tiled=True).reshape(slots, features)

    table = jnp.concatenate([passage_low, exchange(matmul(select, passage_low, 0, 0))], axis=0)

    scored = []
    for (first, last), piece in zip(starts, gathered):
        piece_rows = last - first
        count = dp_count * piece_rows
        row = jnp.arange(count)[:, None]
        local = wanting - first
        target = jnp.where((local >= 0) & (local < piece_rows), wanting_dp * piece_rows + local, -1)
        mine = jnp.arange(row_count) - first
        positive = jnp.where((mine >= 0) & (mine < piece_rows), me * piece_rows + mine, -1)
        positive = row == jnp.pad(positive, (0, slots), constant_values=-1)[None, :]
        masked = (row != jnp.pad(target, (row_count, 0))[None, :]) & (jnp.arange(row_count + slots)[None, :] >= row_count)
        scores = jnp.where(masked, -jnp.inf, matmul(piece, table, 1, 1) * inverse_temp)
        highest = jnp.max(scores, axis=1)
        scored.append((scores, positive, highest, jnp.sum(jnp.exp(scores - highest[:, None]), axis=1)))
    stats = jnp.stack([jnp.concatenate([x[i] for x in scored]) for i in (2, 3)])
    stats = jnp.broadcast_to(stats[None], (dp_count,) + stats.shape)
    stats = lax.all_to_all(stats, "dp", split_axis=0, concat_axis=0, tiled=True)
    highest = jnp.max(stats[:, 0], axis=0)
    normals = highest + jnp.log(jnp.sum(stats[:, 1] * jnp.exp(stats[:, 0] - highest[None, :]), axis=0))
    weights, losses, shares, start = [], [], [], 0
    for (first, last), (scores, positive, _, _) in zip(starts, scored):
        normal = normals[start : start + scores.shape[0]]
        start += scores.shape[0]
        loss = normal - jnp.sum(jnp.where(positive, scores, 0.0), axis=1)
        losses.append(lax.dynamic_slice_in_dim(loss, me * (last - first), last - first, axis=0))
        weight = (jnp.exp(scores - normal[:, None]) - positive.astype(jnp.float32)).astype(jnp.bfloat16)
        weights.append(weight)
        shares.append((matmul(weight, table, 1, 0) * inverse_temp).astype(jnp.bfloat16))
    query_grad = [
        lax.psum_scatter(shares[0], "dp", scatter_dimension=0, tiled=True),
        scatter_end(*scatter_begin(shares[1], me, dp_count), dp_count),
    ]

    weights = jnp.concatenate(weights, axis=0)
    everything = jnp.concatenate(gathered, axis=0)
    passage_grad = matmul(weights[:, :row_count], everything, 0, 0)
    hard_grad = matmul(weights[:, row_count:], everything, 0, 0) * inverse_temp
    passage_grad = passage_grad * inverse_temp + matmul(select, exchange(hard_grad), 1, 0)
    early, late = query_grad
    query_grad = jnp.pad(late, ((ahead, 0), (0, 0)))
    query_grad, early, passage_grad = lax.optimization_barrier((query_grad, early, passage_grad))
    query_grad = lax.dynamic_update_slice(query_grad, early.astype(jnp.float32), (0, 0))
    return (query_grad[None], passage_grad[None], jnp.concatenate(losses)[None])


def solution(mesh):
    return jax.shard_map(
        per_device,
        mesh=mesh,
        in_specs=(P("group", "dp", None), P("group", "dp", None), P("group", "dp", None)),
        out_specs=(P("group", "dp", None), P("group", "dp", None), P("group", "dp")),
        check_vma=False,
    )
```

```python
import jax
import jax.numpy as jnp
from jax import lax
from jax.sharding import PartitionSpec as P

inverse_temp = 50.0
later_part = 8


def ways(step, count):
    return [(i, i + 1) for i in range(step - 1, count - 1)], [(i + 1, i) for i in range(count - step)]


def send_direct(block, count):
    return [lax.ppermute(block, "dp", [(i, (i + step) % count) for i in range(count)]) for step in range(1, count)]


def in_order(block, moved, me, count):
    rows = block.shape[0]
    whole = jnp.zeros((rows * count, block.shape[1]), block.dtype)
    for step, x in enumerate([block] + moved):
        whole = lax.dynamic_update_slice_in_dim(whole, x, (me - step) % count * rows, axis=0)
    return whole


def scatter_begin(share, me, count):
    rows = share.shape[0] // count

    def part(index):
        return lax.dynamic_slice_in_dim(share, index * rows, rows, axis=0)

    terms = [part(me)]
    up, down = None, None
    for step in range(max(count - 2, 1), 0, -1):
        low, high = part((me - step) % count), part((me + step) % count)
        if up is not None:
            low = low.astype(jnp.float32), down
            high = high.astype(jnp.float32), up
        if step > 1:
            above, below = ways(step, count)
            if up is not None:
                low, high = (added(*x) for x in (low, high))
            down = lax.ppermute(low, "dp", [(j, i) for i, j in above])
            up = lax.ppermute(high, "dp", [(j, i) for i, j in below])
    if count > 2:
        terms.append(lax.ppermute(part(count - 1 - me), "dp", [(0, count - 1), (count - 1, 0)]))
    return terms, low, high


def added(kept, came):
    return (kept + came.astype(jnp.float32)).astype(jnp.bfloat16)


def scatter_end(terms, low, high, count):
    low, high = (added(*x) if isinstance(x, tuple) else x for x in (low, high))
    above, below = ways(1, count)
    down = lax.ppermute(low, "dp", [(j, i) for i, j in above])
    up = lax.ppermute(high, "dp", [(j, i) for i, j in below])
    return sum(term.astype(jnp.float32) for term in terms + [up, down])


def matmul(a, b, left, right):
    return lax.dot_general(a, b, (((left,), (right,)), ((), ())), preferred_element_type=jnp.float32)


def per_device(queries, passages, hard_ids):
    row_count, features = queries.shape[1:]
    hard = hard_ids.shape[2]
    dp_count = lax.axis_size("dp")
    group_count = lax.axis_size("group")
    devices = dp_count * group_count
    me = lax.axis_index("dp")
    my_group = lax.axis_index("group")
    batch_rows = row_count * dp_count
    entries = row_count * hard
    capacity = (entries + devices - 1) // devices
    slots = devices * capacity

    ahead = row_count - row_count // later_part
    query_ahead = queries[0, :ahead].astype(jnp.bfloat16)
    query_later = lax.optimization_barrier(queries[0, ahead:]).astype(jnp.bfloat16)
    passage_low = passages[0].astype(jnp.bfloat16)

    piece_ahead = lax.all_gather(query_ahead, "dp", axis=0, tiled=True)
    piece_later = in_order(query_later, send_direct(query_later, dp_count), me, dp_count)
    gathered = [piece_ahead, piece_later]
    starts = [(0, ahead), (ahead, row_count)]

    ids = hard_ids[0].T.reshape(entries)
    owner_group = ids // batch_rows
    owner_dp = ids % batch_rows // row_count
    owner = owner_dp * group_count + owner_group
    order = jnp.arange(entries)
    earlier = (order[None, :] < order[:, None]) & (owner[None, :] == owner[:, None])
    rank = jnp.sum(earlier.astype(jnp.int32), axis=1)
    slot = owner * capacity + rank
    placed = jnp.arange(slots)[:, None] == slot[None, :]
    query_row = jnp.sum(jnp.where(placed, order[None, :] % row_count + 1, 0), axis=1) - 1
    passage_row = jnp.sum(jnp.where(placed, ids[None, :] % row_count + 1, 0), axis=1) - 1

    plane = group_count * capacity
    request = jnp.concatenate(
        [
            passage_row.reshape(dp_count, group_count, capacity),
            jnp.broadcast_to(query_row.reshape(dp_count, 1, plane), (dp_count, group_count, plane)),
        ],
        axis=2,
    ).reshape(devices, capacity + plane)
    request = lax.all_to_all(request, ("dp", "group"), split_axis=0, concat_axis=0, tiled=True)
    request = request.reshape(dp_count, group_count, capacity + plane)
    sent_row = request[:, :, :capacity].transpose(1, 0, 2).reshape(slots)
    wanting = lax.dynamic_index_in_dim(request[:, :, capacity:], my_group, axis=1, keepdims=False)
    wanting = wanting.reshape(dp_count, group_count, capacity).transpose(1, 0, 2).reshape(slots)
    wanting_dp = jnp.arange(slots) // capacity % dp_count

    select = (jnp.arange(row_count)[:, None] == sent_row[None, :]).astype(jnp.bfloat16)

    def exchange(rows):
        rows = rows.astype(jnp.bfloat16).reshape(group_count, dp_count * capacity, features)
        return lax.all_to_all(rows, "group", split_axis=0, concat_axis=0, tiled=True).reshape(slots, features)

    table = jnp.concatenate([passage_low, exchange(matmul(select, passage_low, 0, 0))], axis=0)

    scored = []
    for (first, last), piece in zip(starts, gathered):
        piece_rows = last - first
        count = dp_count * piece_rows
        row = jnp.arange(count)[:, None]
        local = wanting - first
        target = jnp.where((local >= 0) & (local < piece_rows), wanting_dp * piece_rows + local, -1)
        mine = jnp.arange(row_count) - first
        positive = jnp.where((mine >= 0) & (mine < piece_rows), me * piece_rows + mine, -1)
        positive = row == jnp.pad(positive, (0, slots), constant_values=-1)[None, :]
        masked = (row != jnp.pad(target, (row_count, 0))[None, :]) & (jnp.arange(row_count + slots)[None, :] >= row_count)
        scores = jnp.where(masked, -jnp.inf, matmul(piece, table, 1, 1) * inverse_temp)
        highest = jnp.max(scores, axis=1)
        scored.append((scores, positive, highest, jnp.sum(jnp.exp(scores - highest[:, None]), axis=1)))
    stats = jnp.stack([jnp.concatenate([x[i] for x in scored]) for i in (2, 3)])
    stats = jnp.broadcast_to(stats[None], (dp_count,) + stats.shape)
    stats = lax.all_to_all(stats, "dp", split_axis=0, concat_axis=0, tiled=True)
    highest = jnp.max(stats[:, 0], axis=0)
    normals = highest + jnp.log(jnp.sum(stats[:, 1] * jnp.exp(stats[:, 0] - highest[None, :]), axis=0))
    weights, losses, shares, start = [], [], [], 0
    for (first, last), (scores, positive, _, _) in zip(starts, scored):
        normal = normals[start : start + scores.shape[0]]
        start += scores.shape[0]
        loss = normal - jnp.sum(jnp.where(positive, scores, 0.0), axis=1)
        losses.append(lax.dynamic_slice_in_dim(loss, me * (last - first), last - first, axis=0))
        weight = (jnp.exp(scores - normal[:, None]) - positive.astype(jnp.float32)).astype(jnp.bfloat16)
        weights.append(weight)
        shares.append((matmul(weight, table, 1, 0) * inverse_temp).astype(jnp.bfloat16))
    query_grad = [
        lax.psum_scatter(shares[0], "dp", scatter_dimension=0, tiled=True),
        scatter_end(*scatter_begin(shares[1], me, dp_count), dp_count),
    ]

    weights = jnp.concatenate(weights, axis=0)
    everything = jnp.concatenate(gathered, axis=0)
    passage_grad = matmul(weights[:, :row_count], everything, 0, 0)
    hard_grad = matmul(weights[:, row_count:], everything, 0, 0) * inverse_temp
    passage_grad = passage_grad * inverse_temp + matmul(select, exchange(hard_grad), 1, 0)
    early, late = query_grad
    query_grad = jnp.pad(late, ((ahead, 0), (0, 0)))
    query_grad, early, passage_grad = lax.optimization_barrier((query_grad, early, passage_grad))
    query_grad = lax.dynamic_update_slice(query_grad, early.astype(jnp.float32), (0, 0))
    return (query_grad[None], passage_grad[None], jnp.concatenate(losses)[None])


def solution(mesh):
    return jax.shard_map(
        per_device,
        mesh=mesh,
        in_specs=(P("group", "dp", None), P("group", "dp", None), P("group", "dp", None)),
        out_specs=(P("group", "dp", None), P("group", "dp", None), P("group", "dp")),
        check_vma=False,
    )
```
